128 devices in a mesh: seq: 16 (over z, y), head: 2 (over core), clip: 4 (over x).
Axes of the slice: x: 4, y: 4, z: 4, core: 2. Of those that a mesh axis runs over, the one named last changes fastest.
Arguments:
- queries: bfloat16 [4, 2048, 2560], P('clip', 'seq', 'head'), may hold values from -5000 to 5000
- keys: bfloat16 [4, 2048, 2560], P('clip', 'seq', 'head'), may hold values from -5000 to 5000
- values: bfloat16 [4, 2048, 2560], P('clip', 'seq', 'head'), may hold values from -6 to 6
- q_gain: float32 [2560], P('head'), may hold values from 0.25 to 1.75
- k_gain: float32 [2560], P('head'), may hold values from 0.25 to 1.75
- clip_frames: int32 [4, 8], P('clip'), may hold values from 1 to 36, 64 in all within a row
- out_weight: bfloat16 [2560, 5120], P('head', 'clip'), may hold values from -0.125 to 0.125
Outputs:
- attended: bfloat16 [4, 2048, 2560], P('clip', 'seq', 'head')
- projected: bfloat16 [4, 2048, 5120], P('clip', 'seq', 'head')
The draws below stay inside these ranges and needn't reach their ends.
Inputs may be any that keep to these rules, and one draw needn't show every extreme that they name: `clip_frames`: each row holds 8 lengths summing to 64; the longest is exactly 36.
All inputs are finite; a program needn't handle non-finite values.
Results may differ from the reference program's by a relative error of at most 0.0098.
Values may be sent and summed in bfloat16 or wider, within the bound.
A program may use at most 128 MiB of HBM per device.

```python
import math
import jax
import jax.numpy as jnp
import numpy as np
from jax import lax

HEADS = 20
HEAD_DIM = 128
DIM = 5120
TOK_FRAME = 32
HD = 2560
FRAMES = 64
SEQ_LEN = 2048
CLIPS = 8
MOST_FR = 36
N_CLIP = 4


def query_key_pair(key):
    keys_all = jax.random.split(key, 5)
    shape = (N_CLIP, SEQ_LEN, HD)
    columns = jnp.exp(jax.random.uniform(keys_all[2], (HD,), minval=0.0, maxval=math.log(10.0)))
    base_q = jnp.clip(jax.random.normal(keys_all[0], shape), -5.0, 5.0)
    base_k = jnp.clip(jax.random.normal(keys_all[1], shape), -5.0, 5.0)
    rows_q = jnp.exp(jax.random.uniform(keys_all[3], (N_CLIP, SEQ_LEN, 1), minval=0.0, maxval=math.log(10.0)))
    rows_k = jnp.exp(jax.random.uniform(keys_all[4], (N_CLIP, SEQ_LEN, 1), minval=0.0, maxval=math.log(10.0)))
    made_q = base_q * columns * rows_q
    made_k = base_k * columns * rows_k
    return (made_q, made_k)


def draw_queries(key, part):
    made_q, made_k = query_key_pair(key)
    return made_q.astype(jnp.bfloat16)


def draw_keys(key, part):
    made_q, made_k = query_key_pair(key)
    return made_k.astype(jnp.bfloat16)


def block_levels(key, extent, cuts, least, largest):
    def one(dim, blocks):
        steps = jax.random.uniform(jax.random.fold_in(jax.random.fold_in(key, 6), dim), (blocks,), jnp.float32, least / len(cuts), largest / len(cuts))
        return jnp.repeat(jnp.exp(steps), extent[dim] // blocks).reshape((-1,) + (1,) * (len(extent) - dim - 1))

    level = one(*cuts[0])
    for cut in cuts[1:]:
        level = level * one(*cut)
    return level


def profile(count, total, limit, slope):
    loads = [(1 << 20) // math.isqrt(standing ** slope) + 1 for standing in range(2, count + 1)]
    spare, holding = total - limit - (count - 1), [1] * (count - 1)
    while spare > 0:
        candidates = [i for i in range(count - 1) if holding[i] < limit]
        whole, left = sum([loads[i] for i in candidates]), spare
        for i in candidates:
            more = min(limit - holding[i], max(1, left * loads[i] // whole), spare)
            holding[i] = holding[i] + more
            spare = spare - more
    return np.array([limit] + holding)


def uneven(stream_key, number_of, total, bound, slope):
    if number_of == 2:
        one = jax.random.randint(stream_key, (), max(1, total - bound), min(bound, total - 1) + 1)
        return jnp.stack([one, total - one])
    sizes = jnp.asarray(profile(number_of, total, bound, slope), jnp.int32)
    couples = (number_of - 1) // 2
    giver, sink = sizes[1:1 + 2 * couples:2], sizes[2:2 + 2 * couples:2]
    room = jnp.minimum(giver - 1, bound - sink)
    shifted = jax.random.randint(jax.random.fold_in(stream_key, 1), (couples,), 0, 1 << 20) % (room + 1)
    sizes = sizes.at[1:1 + 2 * couples:2].set(giver - shifted).at[2:2 + 2 * couples:2].set(sink + shifted)
    return sizes[jax.random.permutation(jax.random.fold_in(stream_key, 2), number_of)]


def bell_draw(key, dims, scale, limit, pieces=(), kind=jnp.bfloat16):
    array = scale * jax.random.normal(key, dims, jnp.float32)
    if pieces:
        array = array * block_levels(key, dims, pieces, -0.22, 0.18)
    return jnp.clip(array, -limit, limit).astype(kind)


def setup_inputs(seed: int = 0) -> dict:
    splits = jax.random.split(jax.random.key(seed), 8)
    queries = draw_queries(jax.random.fold_in(splits[7], 71), 0)
    keys = draw_keys(jax.random.fold_in(splits[7], 71), 0)
    values = bell_draw(splits[2], (N_CLIP, SEQ_LEN, HD), 1.0, 6.0, ((0, 4), (1, 16), (2, 2)))
    q_gain = jnp.clip(1.0 + 0.15 * jax.random.normal(splits[3], (HD,), jnp.float32), 0.25, 1.75)
    k_gain = jnp.clip(1.0 + 0.15 * jax.random.normal(splits[4], (HD,), jnp.float32), 0.25, 1.75)
    clip_frames = jax.vmap(lambda own: uneven(own, CLIPS, FRAMES, MOST_FR, 2))(jax.random.split(splits[5], N_CLIP)).reshape((N_CLIP, CLIPS)).astype(jnp.int32)
    out_weight = bell_draw(splits[6], (HD, DIM), HD ** -0.5, 0.125, ((0, 2), (1, 4)))
    return dict(queries=queries, keys=keys, values=values, q_gain=q_gain, k_gain=k_gain, clip_frames=clip_frames, out_weight=out_weight)


def frame_ids(lengths_row, count):
    ends = jnp.cumsum(lengths_row.astype(jnp.int32))
    marks = (jnp.arange(count, dtype=jnp.int32)[:, None] >= ends[None, :]).astype(jnp.int32)
    return lax.optimization_barrier(jnp.sum(marks, axis=1)).astype(jnp.int32)

def rms_scale(values_in, gain):
    xf = values_in.astype(jnp.float32)
    return xf * lax.rsqrt(lax.optimization_barrier(jnp.mean(xf * xf, axis=-1, keepdims=True)) + 1e-06) * gain.astype(jnp.float32)

def reference(queries, keys, values, q_gain, k_gain, clip_frames, out_weight):
    q_norm = rms_scale(queries, q_gain).astype(jnp.bfloat16)
    k_norm = rms_scale(keys, k_gain).astype(jnp.bfloat16)
    scale = HEAD_DIM ** (-0.5)
    block = min(512, SEQ_LEN)
    count = SEQ_LEN // block

    def one_group(items):
        q_group, k_group, v_group, lens = items
        token_clip = frame_ids(lens, FRAMES)[jnp.arange(SEQ_LEN, dtype=jnp.int32) // TOK_FRAME]
        k_heads = k_group.reshape(SEQ_LEN, HEADS, HEAD_DIM).astype(jnp.float32)
        v_heads = v_group.reshape(SEQ_LEN, HEADS, HEAD_DIM).astype(jnp.float32)

        def one_block(index):
            start = (index * block).astype(jnp.int32)
            q_block = lax.dynamic_slice_in_dim(q_group, start, block, 0).reshape(block, HEADS, HEAD_DIM)
            ids = lax.dynamic_slice_in_dim(token_clip, start, block, 0)
            score = jnp.einsum('qhd,khd->hqk', q_block.astype(jnp.float32), k_heads) * scale
            same = (ids[:, None] == token_clip[None, :])[None]
            score = jnp.where(same, score, jnp.float32(-1e+30))
            top = lax.optimization_barrier(jnp.max(score, axis=-1, keepdims=True))
            expo = jnp.where(same, jnp.exp(score - top), jnp.float32(0.0))
            total = lax.optimization_barrier(jnp.sum(expo, axis=-1))
            weights = lax.optimization_barrier(expo.astype(jnp.bfloat16))
            summed = jnp.einsum('hqk,khd->qhd', weights.astype(jnp.float32), v_heads)
            return (summed / total.T[:, :, None]).reshape(block, HD).astype(jnp.bfloat16)
        return lax.map(one_block, jnp.arange(count, dtype=jnp.int32)).reshape(SEQ_LEN, HD)
    attended = lax.map(one_group, (q_norm, k_norm, values, clip_frames))
    flat = attended.reshape(N_CLIP * SEQ_LEN, HD)
    projected = jnp.dot(flat, out_weight, preferred_element_type=jnp.float32).reshape(N_CLIP, SEQ_LEN, DIM).astype(jnp.bfloat16)
    return (attended, projected)
```

```python
import jax
import jax.numpy as jnp
from jax import lax
from jax.experimental import pallas as pl
from jax.experimental.pallas import tpu as pltpu
from jax.sharding import PartitionSpec as P

HEADS = 20
HEAD_DIM = 128
HD = HEADS * HEAD_DIM
TOK_FRAME = 32
CLIPS = 8
SEQ = 16
ROWS = 128
WIDE = 1280
HERE = WIDE // HEAD_DIM
CHUNKS = 4
TOKENS = SEQ * ROWS
OUT_HALF = 640
MASKED = -1e30
MESH = pl.DeviceIdType.MESH


def lanes(start, size=HEAD_DIM):
    return pl.ds(pl.multiple_of(start, 128), size)


def rows(start, size):
    return pl.ds(pl.multiple_of(start, 32), size)


def owner_of(core, head):
    turn = head // 4
    z = head % 4 + 2 * core * (head // 8)
    y = (z + turn * (1 + 2 * core)) % 4
    return z * 4 + y


def owned_by(core, place):
    z, y = place // 4, place % 4
    off = (y - z + 4) % 4
    turn = jnp.where(off == 0, 0, jnp.where(off == 2, 2, jnp.where(off == 1 + 2 * core, 1, -1)))
    last = z - 2 * core
    head = jnp.where(turn == 2, 8 + last, turn * 4 + z)
    good = (turn >= 0) & ((turn < 2) | ((last >= 0) & (last < 2)))
    return jnp.where(good, head, -1)


def kernel(
    lens, q_in, k_in, v_in, q_gain, k_gain, w_in, att_out, proj_out,
    qf, kf, qn, kn, sums, qx, kx, vx, back, ag, w2, res,
    load_sem, sum_sem, w_sem, v_sem, k_sem, q_sem, r_sem, x_sem, d_sem, o_sem, a_sem,
    s_sum, s_w, s_v, s_k, s_q, s_r, s_x, s_d, s_o,
):
    place, core, group = lax.axis_index("seq"), lax.axis_index("head"), lax.axis_index("clip")
    other = 1 - core
    mine = owned_by(core, place)
    owner = mine >= 0

    loads = [
        pltpu.make_async_copy(q_in.at[0], qf, load_sem.at[0]),
        pltpu.make_async_copy(k_in.at[0], kf, load_sem.at[1]),
        pltpu.make_async_copy(w_in.at[:, lanes(core * OUT_HALF, OUT_HALF)], w2.at[core], load_sem.at[2]),
    ]
    for load in loads:
        load.start()

    barrier = pltpu.get_barrier_semaphore()

    def greet_plane(i, carry):
        to = (place + i) % SEQ
        pl.semaphore_signal(barrier, inc=1, device_id=(to, core, group), device_id_type=MESH)
        return carry

    lax.fori_loop(1, SEQ, greet_plane, 0)
    pl.semaphore_signal(barrier, inc=1, device_id=(place, other, group), device_id_type=MESH)

    def greet_line(i, carry):
        to = (group + i) % 4
        pl.semaphore_signal(barrier, inc=1, device_id=(place, core, to), device_id_type=MESH)
        pl.semaphore_signal(barrier, inc=1, device_id=(place, other, to), device_id_type=MESH)
        return carry

    lax.fori_loop(1, 4, greet_line, 0)
    pl.semaphore_wait(barrier, SEQ - 1 + 1 + 6)

    def to_owners(copies):
        def one(i, carry):
            head = (i + place) % HERE
            to = owner_of(core, head)

            @pl.when(to == place)
            def _():
                for src, dst, send, recv in copies(head):
                    pltpu.make_async_copy(src, dst, recv).start()

            @pl.when(to != place)
            def _():
                for src, dst, send, recv in copies(head):
                    pltpu.make_async_remote_copy(
                        src, dst, send, recv, device_id=(to, core, group), device_id_type=MESH
                    ).start()

            return carry

        lax.fori_loop(0, HERE, one, 0)

    own_rows = rows(place * ROWS, ROWS)
    to_owners(lambda head: [(v_in.at[0, :, lanes(head * 128)], vx.at[own_rows, pl.ds(0, 128)], s_v, v_sem)])

    loads[0].wait()
    loads[1].wait()
    q_float = qf[...].astype(jnp.float32)
    k_float = kf[...].astype(jnp.float32)
    sum_q = jnp.sum(q_float * q_float, axis=1, keepdims=True)
    sum_k = jnp.sum(k_float * k_float, axis=1, keepdims=True)
    low = lax.broadcasted_iota(jnp.int32, (ROWS, 128), 1) < 64
    sums[0] = jnp.where(low, sum_q, sum_k)
    give_sums = pltpu.make_async_remote_copy(
        sums.at[0], sums.at[1], s_sum, sum_sem, device_id=(place, other, group), device_id_type=MESH
    )
    give_sums.start()
    give_w = pltpu.make_async_remote_copy(
        w_in.at[:, lanes(other * OUT_HALF, OUT_HALF)], w2.at[core], s_w, w_sem,
        device_id=(place, other, group), device_id_type=MESH,
    )
    give_w.start()
    give_sums.wait()
    both = sums[0] + sums[1]
    k_rate = lax.rsqrt(both[:, 64:65] / HD + 1e-06)
    kn[...] = (kf[...].astype(jnp.float32) * k_rate * k_gain[...]).astype(jnp.bfloat16)
    to_owners(lambda head: [(kn.at[:, lanes(head * 128)], kx.at[own_rows, pl.ds(0, 128)], s_k, k_sem)])
    q_rate = lax.rsqrt(both[:, 0:1] / HD + 1e-06)
    qn[...] = (qf[...].astype(jnp.float32) * q_rate * q_gain[...]).astype(jnp.bfloat16)

    def send_q(chunk, carry):
        to_owners(
            lambda head: [
                (
                    qn.at[rows(chunk * 32, 32), lanes(head * 128)],
                    qx.at[chunk, rows(place * 32, 32), pl.ds(0, 128)],
                    s_q,
                    q_sem.at[chunk],
                )
            ]
        )
        return carry

    lax.fori_loop(0, CHUNKS, send_q, 0)

    @pl.when(owner)
    def _():
        lane = lax.broadcasted_iota(jnp.int32, (1, 128), 1)
        first = jnp.zeros((1, 128), jnp.int32)
        last = jnp.zeros((1, 128), jnp.int32)
        end = jnp.int32(0)
        for clip in range(CLIPS):
            first = jnp.where(lane == clip, end, first)
            end = end + lens[0, clip]
            last = jnp.where(lane == clip, end, last)
        one = jnp.ones((), jnp.float32)
        zero = jnp.zeros((), jnp.float32)
        frame = lax.broadcasted_iota(jnp.int32, (TOKENS, 128), 0) // TOK_FRAME
        kx[:, 128:256] = jnp.where((frame >= first) & (frame < last), one, zero).astype(jnp.bfloat16)
        vx[:, 128:256] = jnp.ones((TOKENS, 128), jnp.bfloat16)
        for chunk in range(CHUNKS):
            frame = lax.broadcasted_iota(jnp.int32, (SEQ * 32, 128), 0) // 32 * CHUNKS + chunk
            off = jnp.logical_not((frame >= first) & (frame < last)) & (lane < CLIPS)
            qx[chunk, :, 128:256] = jnp.where(off, MASKED * one, zero).astype(jnp.bfloat16)
        pltpu.make_async_copy(vx.at[:, pl.ds(0, 128)], vx.at[:, pl.ds(0, 128)], v_sem).wait()
        pltpu.make_async_copy(kx.at[:, pl.ds(0, 128)], kx.at[:, pl.ds(0, 128)], k_sem).wait()

    loads[2].wait()
    give_w.wait()
    factor = HEAD_DIM ** (-0.5) * 1.4426950408889634

    def step(t, carry):
        @pl.when(owner & (t < CHUNKS))
        def _():
            chunk = t
            pltpu.make_async_copy(
                qx.at[chunk, :, pl.ds(0, 128)], qx.at[chunk, :, pl.ds(0, 128)], q_sem.at[chunk]
            ).wait()

            def attend(part, carry):
                span = rows(part * 256, 256)
                score = lax.dot_general(
                    qx[chunk, span, :], kx[...], (((1,), (1,)), ((), ())), preferred_element_type=jnp.float32
                )
                top = jnp.max(score, axis=1, keepdims=True)
                weights = jnp.exp2((score - top) * factor).astype(jnp.bfloat16)
                summed = jnp.dot(weights, vx[...], preferred_element_type=jnp.float32)
                back[chunk, span, :] = (summed[:, :128] / summed[:, 128:]).astype(jnp.bfloat16)
                return carry

            lax.fori_loop(0, 2, attend, 0)

            def give(i, carry):
                to = (place + i) % SEQ
                src = back.at[chunk, rows(to * 32, 32)]
                dst = ag.at[chunk, core, rows(group * 32, 32), lanes(mine * 128)]

                @pl.when(i == 0)
                def _():
                    pltpu.make_async_copy(src, dst, r_sem.at[chunk]).start()

                @pl.when(i > 0)
                def _():
                    pltpu.make_async_remote_copy(
                        src, dst, s_r, r_sem.at[chunk], device_id=(to, core, group), device_id_type=MESH
                    ).start()

                return carry

            lax.fori_loop(0, SEQ, give, 0)

        @pl.when((t >= 1) & (t < CHUNKS + 1))
        def _():
            chunk = t - 1
            block = ag.at[chunk, core, rows(group * 32, 32)]
            pltpu.make_async_copy(block, block, r_sem.at[chunk]).wait()
            for i in range(1, 4):
                pltpu.make_async_remote_copy(
                    block, block, s_x, x_sem.at[chunk],
                    device_id=(place, core, (group + i) % 4), device_id_type=MESH,
                ).start()
            pltpu.make_async_remote_copy(
                block, block, s_d, d_sem.at[chunk], device_id=(place, other, group), device_id_type=MESH
            ).start()
            pltpu.make_async_copy(block, att_out.at[0, rows(chunk * 32, 32)], a_sem).start()

        @pl.when((t >= 2) & (t < CHUNKS + 2))
        def _():
            chunk = t - 2
            three = ag.at[chunk, core, pl.ds(0, 96)]
            pltpu.make_async_copy(three, three, x_sem.at[chunk]).wait()
            for i in range(1, 4):
                block = ag.at[chunk, core, rows((group + i) % 4 * 32, 32)]
                pltpu.make_async_remote_copy(
                    block, block, s_d, d_sem.at[chunk], device_id=(place, other, group), device_id_type=MESH
                ).start()

        @pl.when(t >= 3)
        def _():
            chunk = t - 3
            half = ag.at[chunk, other]
            pltpu.make_async_copy(half, half, d_sem.at[chunk]).wait()
            total = jnp.dot(ag[chunk, 0], w2[0], preferred_element_type=jnp.float32)
            total += jnp.dot(ag[chunk, 1], w2[1], preferred_element_type=jnp.float32)
            res[chunk] = total.astype(jnp.bfloat16)
            to_core = group // 2
            dst = proj_out.at[0, rows(chunk * 32, 32), lanes((group % 2) * WIDE + core * OUT_HALF, OUT_HALF)]
            for i in range(4):
                to = (group + i) % 4
                src = res.at[chunk, rows(to * 32, 32)]

                def far(src=src, to=to):
                    pltpu.make_async_remote_copy(
                        src, dst, s_o, o_sem, device_id=(place, to_core, to), device_id_type=MESH
                    ).start()

                if i:
                    far()
                else:
                    pl.when(to_core != core)(far)

                    @pl.when(to_core == core)
                    def _(src=src):
                        pltpu.make_async_copy(src, dst, o_sem).start()

        return carry

    lax.fori_loop(0, CHUNKS + 3, step, 0)

    def done(ref, sem):
        pltpu.make_async_copy(ref, ref, sem).wait()

    @pl.when(owner)
    def _():
        for sem in (s_v, s_k, s_q):
            done(kn.at[:, pl.ds(0, 9 * 128)], sem)
        done(kx.at[pl.ds(0, TOKENS - ROWS), pl.ds(0, 128)], s_r)

    @pl.when(jnp.logical_not(owner))
    def _():
        for sem in (s_v, s_k, s_q):
            done(kn, sem)

    done(ag.at[pl.ds(0, 3), 0], s_x)
    done(ag.at[:, 0], s_d)

    @pl.when(group // 2 == core)
    def _():
        done(res.at[pl.ds(0, 3)], s_o)

    @pl.when(group // 2 != core)
    def _():
        done(res, s_o)

    done(att_out, a_sem)
    done(proj_out, o_sem)


def body(queries, keys, values, q_gain, k_gain, clip_frames, out_weight):
    anywhere = pl.BlockSpec(memory_space=pl.ANY)
    vmem = pl.BlockSpec(memory_space=pltpu.VMEM)
    bf16, f32 = jnp.bfloat16, jnp.float32
    dma = pltpu.SemaphoreType.DMA
    return pl.pallas_call(
        kernel,
        out_shape=(
            jax.ShapeDtypeStruct((1, ROWS, WIDE), bf16),
            jax.ShapeDtypeStruct((1, ROWS, 2 * WIDE), bf16),
        ),
        in_specs=[pl.BlockSpec(memory_space=pltpu.SMEM), anywhere, anywhere, anywhere, vmem, vmem, anywhere],
        out_specs=(anywhere, anywhere),
        scratch_shapes=[
            pltpu.VMEM((ROWS, WIDE), bf16),
            pltpu.VMEM((ROWS, WIDE), bf16),
            pltpu.VMEM((ROWS, WIDE), bf16),
            pltpu.VMEM((ROWS, WIDE), bf16),
            pltpu.VMEM((2, ROWS, 128), f32),
            pltpu.VMEM((CHUNKS, SEQ * 32, 256), bf16),
            pltpu.VMEM((TOKENS, 256), bf16),
            pltpu.VMEM((TOKENS, 256), bf16),
            pltpu.VMEM((CHUNKS, SEQ * 32, 128), bf16),
            pltpu.VMEM((CHUNKS, 2, 128, WIDE), bf16),
            pltpu.VMEM((2, WIDE, OUT_HALF), bf16),
            pltpu.VMEM((CHUNKS, 128, OUT_HALF), bf16),
            dma((3,)), dma, dma, dma, dma, dma((CHUNKS,)), dma((CHUNKS,)), dma((CHUNKS,)), dma((CHUNKS,)), dma, dma,
            dma, dma, dma, dma, dma, dma, dma, dma, dma,
        ],
        compiler_params=pltpu.CompilerParams(
            collective_id=0, has_side_effects=True, vmem_limit_bytes=56 << 20
        ),
        cost_estimate=pl.CostEstimate(flops=3 * 10**9, bytes_accessed=8 << 20, transcendentals=4 << 20),
    )(clip_frames, queries, keys, values, q_gain[None], k_gain[None], out_weight)


def solution(mesh):
    in_specs = (
        P("clip", "seq", "head"),
        P("clip", "seq", "head"),
        P("clip", "seq", "head"),
        P("head"),
        P("head"),
        P("clip", None),
        P("head", "clip"),
    )
    out_specs = (P("clip", "seq", "head"), P("clip", "seq", "head"))
    return jax.shard_map(body, mesh=mesh, in_specs=in_specs, out_specs=out_specs, check_vma=False)
```

```python
import jax
import jax.numpy as jnp
from jax import lax
from jax.experimental import pallas as pl
from jax.experimental.pallas import tpu as pltpu
from jax.sharding import PartitionSpec as P

HEADS = 20
HEAD_DIM = 128
HD = HEADS * HEAD_DIM
TOK_FRAME = 32
CLIPS = 8
SEQ = 16
ROWS = 128
WIDE = 1280
HERE = WIDE // HEAD_DIM
PART = 16
CHUNKS = ROWS // PART
SLOTS = CHUNKS // 2
BLOCK = SEQ * PART
KEYS = 512
TOKENS = SEQ * ROWS
LAG_HOME, LAG_LINE, LAG_OUT = 3, 6, 11
MASKED = -1e30
MESH = pl.DeviceIdType.MESH


def lanes(start, size=HEAD_DIM):
    return pl.ds(pl.multiple_of(start, 128), size)


def rows(start, size):
    return pl.ds(pl.multiple_of(start, 16), size)


def owner_of(core, head):
    turn = head // 4
    z = head % 4 + 2 * core * (head // 8)
    y = (z + turn * (1 + 2 * core)) % 4
    return z * 4 + y


def owned_by(core, place):
    z, y = place // 4, place % 4
    off = (y - z + 4) % 4
    turn = jnp.where(off == 0, 0, jnp.where(off == 2, 2, jnp.where(off == 1 + 2 * core, 1, -1)))
    last = z - 2 * core
    head = jnp.where(turn == 2, 8 + last, turn * 4 + z)
    good = (turn >= 0) & ((turn < 2) | ((last >= 0) & (last < 2)))
    return jnp.where(good, head, -1)


def kernel(
    lens, q_in, k_in, v_in, q_gain, k_gain, w_in, att_out, proj_out,
    qf, kf, qn, kn, sums, qx, kx, vx, back, ag, w2, res,
    load_sem, sum_sem, w_sem, v_sem, k_sem, q_sem, r_sem, left_sem, right_sem, far_sem, o_sem, a_sem,
    s_sum, s_w, s_v, s_k, s_q, s_r, s_x, s_f, s_o, s_a,
):
    place, core, group = lax.axis_index("seq"), lax.axis_index("head"), lax.axis_index("clip")
    other = 1 - core
    mine = owned_by(core, place)
    owner = mine >= 0

    loads = [
        pltpu.make_async_copy(q_in.at[0], qf, load_sem.at[0]),
        pltpu.make_async_copy(k_in.at[0], kf, load_sem.at[1]),
        pltpu.make_async_copy(w_in, w2.at[rows(core * WIDE, WIDE)], load_sem.at[2]),
    ]
    for load in loads:
        load.start()

    barrier = pltpu.get_barrier_semaphore()

    def greet_plane(i, carry):
        to = (place + i) % SEQ
        pl.semaphore_signal(barrier, inc=1, device_id=(to, core, group), device_id_type=MESH)
        return carry

    lax.fori_loop(1, SEQ, greet_plane, 0)
    pl.semaphore_signal(barrier, inc=1, device_id=(place, other, group), device_id_type=MESH)

    left, right = (group + 3) % 4, (group + 1) % 4
    for to in (left, right):
        pl.semaphore_signal(barrier, inc=1, device_id=(place, core, to), device_id_type=MESH)
    loads[0].wait()
    loads[1].wait()
    q_float = qf[...].astype(jnp.float32)
    k_float = kf[...].astype(jnp.float32)
    sum_q = jnp.sum(q_float * q_float, axis=1, keepdims=True)
    sum_k = jnp.sum(k_float * k_float, axis=1, keepdims=True)
    low = lax.broadcasted_iota(jnp.int32, (ROWS, 128), 1) < 64
    sums[0] = jnp.where(low, sum_q, sum_k)
    pl.semaphore_wait(barrier, SEQ - 1 + 1 + 2)

    def to_owners(copies):
        def one(i, carry):
            head = (i + place) % HERE
            to = owner_of(core, head)

            @pl.when(to == place)
            def _():
                for src, dst, send, recv in copies(head):
                    pltpu.make_async_copy(src, dst, recv).start()

            @pl.when(to != place)
            def _():
                for src, dst, send, recv in copies(head):
                    pltpu.make_async_remote_copy(
                        src, dst, send, recv, device_id=(to, core, group), device_id_type=MESH
                    ).start()

            return carry

        lax.fori_loop(0, HERE, one, 0)

    own_rows = rows(place * ROWS, ROWS)
    to_owners(lambda head: [(v_in.at[0, :, lanes(head * 128)], vx.at[own_rows, pl.ds(0, 128)], s_v, v_sem)])

    give_sums = pltpu.make_async_remote_copy(
        sums.at[0], sums.at[1], s_sum, sum_sem, device_id=(place, other, group), device_id_type=MESH
    )
    give_sums.start()
    give_w = pltpu.make_async_remote_copy(
        w_in, w2.at[rows(core * WIDE, WIDE)], s_w, w_sem,
        device_id=(place, other, group), device_id_type=MESH,
    )
    give_w.start()
    give_sums.wait()
    both = sums[0] + sums[1]
    k_rate = lax.rsqrt(both[:, 64:65] / HD + 1e-06)
    kn[...] = (kf[...].astype(jnp.float32) * k_rate * k_gain[...].reshape(1, WIDE)).astype(jnp.bfloat16)
    to_owners(lambda head: [(kn.at[:, lanes(head * 128)], kx.at[own_rows, pl.ds(0, 128)], s_k, k_sem)])
    q_rate = lax.rsqrt(both[:, 0:1] / HD + 1e-06)
    qn[...] = (qf[...].astype(jnp.float32) * q_rate * q_gain[...].reshape(1, WIDE)).astype(jnp.bfloat16)

    def send_q(chunk, carry):
        to_owners(
            lambda head: [
                (
                    qn.at[rows(chunk * PART, PART), lanes(head * 128)],
                    qx.at[chunk, rows(place * PART, PART), pl.ds(0, 128)],
                    s_q,
                    q_sem.at[chunk],
                )
            ]
        )
        return carry

    lax.fori_loop(0, CHUNKS, send_q, 0)

    @pl.when(owner)
    def _():
        lane = lax.broadcasted_iota(jnp.int32, (1, 128), 1)
        first = jnp.zeros((1, 128), jnp.int32)
        last = jnp.zeros((1, 128), jnp.int32)
        end = jnp.int32(0)
        for clip in range(CLIPS):
            first = jnp.where(lane == clip, end, first)
            end = end + lens[0, clip]
            last = jnp.where(lane == clip, end, last)
        one = jnp.ones((), jnp.float32)
        zero = jnp.zeros((), jnp.float32)
        frame = lax.broadcasted_iota(jnp.int32, (TOKENS, 128), 0) // TOK_FRAME
        kx[:, 128:256] = jnp.where((frame >= first) & (frame < last), one, zero).astype(jnp.bfloat16)
        vx[:, 128:256] = jnp.ones((TOKENS, 128), jnp.bfloat16)
        for chunk in range(CHUNKS):
            frame = lax.broadcasted_iota(jnp.int32, (BLOCK, 128), 0) // PART * (ROWS // TOK_FRAME) + chunk * PART // TOK_FRAME
            off = jnp.logical_not((frame >= first) & (frame < last)) & (lane < CLIPS)
            qx[chunk, :, 128:256] = jnp.where(off, MASKED * one, zero).astype(jnp.bfloat16)
        pltpu.make_async_copy(vx.at[:, pl.ds(0, 128)], vx.at[:, pl.ds(0, 128)], v_sem).wait()
        pltpu.make_async_copy(kx.at[:, pl.ds(0, 128)], kx.at[:, pl.ds(0, 128)], k_sem).wait()

    loads[2].wait()
    give_w.wait()
    factor = HEAD_DIM ** (-0.5) * 1.4426950408889634

    def step(t, carry):
        @pl.when(owner & (t < CHUNKS))
        def _():
            chunk = t
            pltpu.make_async_copy(
                qx.at[chunk, :, pl.ds(0, 128)], qx.at[chunk, :, pl.ds(0, 128)], q_sem.at[chunk]
            ).wait()

            queries = qx[chunk]
            best, summed = None, None
            for first in range(0, TOKENS, KEYS):
                span = pl.ds(first, KEYS)
                score = lax.dot_general(
                    queries, kx[span, :], (((1,), (1,)), ((), ())), preferred_element_type=jnp.float32
                )
                top = jnp.max(score, axis=1, keepdims=True)
                if first:
                    top = jnp.maximum(best, top)
                weights = jnp.exp2((score - top) * factor).astype(jnp.bfloat16)
                added = jnp.dot(weights, vx[span, :], preferred_element_type=jnp.float32)
                summed = summed * jnp.exp2((best - top) * factor) + added if first else added
                best = top
            back[chunk] = (summed[:, :128] / summed[:, 128:]).astype(jnp.bfloat16)

            to_core = chunk % 2

            def give(i, carry):
                to = (place + i) % SEQ
                src = back.at[chunk, rows(to * PART, PART)]
                dst = ag.at[chunk // 2, rows(group * PART, PART), lanes((core * HERE + mine) * 128)]
                here = (i == 0) & (to_core == core)

                @pl.when(here)
                def _():
                    pltpu.make_async_copy(src, dst, r_sem.at[chunk // 2]).start()

                @pl.when(jnp.logical_not(here))
                def _():
                    pltpu.make_async_remote_copy(
                        src, dst, s_r, r_sem.at[chunk // 2], device_id=(to, to_core, group), device_id_type=MESH
                    ).start()

                return carry

            lax.fori_loop(0, SEQ, give, 0)

        def slot_of(lag):
            chunk = t - lag
            return chunk // 2, (chunk >= 0) & (chunk < CHUNKS) & (chunk % 2 == core)

        slot_home, now_home = slot_of(LAG_HOME)

        @pl.when(now_home)
        def _():
            block = ag.at[slot_home, rows(group * PART, PART)]
            pltpu.make_async_copy(block, block, r_sem.at[slot_home]).wait()
            for to, sem in ((right, left_sem), (left, right_sem)):
                pltpu.make_async_remote_copy(
                    block, block, s_x, sem.at[slot_home], device_id=(place, core, to), device_id_type=MESH
                ).start()
            rest = att_out.at[0, rows((2 * slot_home + core) * PART, PART)]
            pltpu.make_async_remote_copy(
                block.at[:, lanes(other * WIDE, WIDE)], rest, s_a, a_sem,
                device_id=(place, other, group), device_id_type=MESH,
            ).start()
            pltpu.make_async_copy(block.at[:, lanes(core * WIDE, WIDE)], rest, a_sem).start()

        slot_out, now_out = slot_of(LAG_OUT)

        @pl.when(now_out)
        def _():
            block = ag.at[slot_out, rows((group + 2) % 4 * PART, PART)]
            pltpu.make_async_copy(block, block, far_sem.at[slot_out]).wait()
            total = jnp.dot(ag[slot_out], w2[...], preferred_element_type=jnp.float32)
            res[rows(slot_out * 4 * PART, 4 * PART), :] = total.astype(jnp.bfloat16)
            to_core = group // 2
            dst = proj_out.at[0, rows((2 * slot_out + core) * PART, PART), lanes((group % 2) * WIDE, WIDE)]
            for i in (2, 1, 3, 0):
                to = (group + i) % 4
                src = res.at[rows((slot_out * 4 + to) * PART, PART)]

                def far(src=src, to=to):
                    pltpu.make_async_remote_copy(
                        src, dst, s_o, o_sem, device_id=(place, to_core, to), device_id_type=MESH
                    ).start()

                if i:
                    far()
                else:
                    pl.when(to_core != core)(far)

                    @pl.when(to_core == core)
                    def _(src=src):
                        pltpu.make_async_copy(src, dst, o_sem).start()

        slot_line, now_line = slot_of(LAG_LINE)

        @pl.when(now_line)
        def _():
            for source, to, sem, first in ((left, right, left_sem, 0), (right, left, right_sem, WIDE)):
                block = ag.at[slot_line, rows(source * PART, PART)]
                pltpu.make_async_copy(block, block, sem.at[slot_line]).wait()
                half = block.at[:, pl.ds(first, WIDE)]
                pltpu.make_async_remote_copy(
                    half, half, s_f, far_sem.at[slot_line], device_id=(place, core, to), device_id_type=MESH
                ).start()

        return carry

    lax.fori_loop(0, CHUNKS + LAG_OUT, step, 0)

    def done(ref, sem):
        pltpu.make_async_copy(ref, ref, sem).wait()

    @pl.when(owner)
    def _():
        for sem in (s_v, s_k, s_q):
            done(kn.at[:, pl.ds(0, 9 * 128)], sem)
        done(kx.at[pl.ds(0, TOKENS - ROWS // 2), pl.ds(0, 128)], s_r)

    @pl.when(jnp.logical_not(owner))
    def _():
        for sem in (s_v, s_k, s_q):
            done(kn, sem)

    done(ag.at[:, pl.ds(0, 2 * PART)], s_x)
    done(ag.at[:, pl.ds(0, PART)], s_f)
    done(ag.at[:, pl.ds(0, PART), pl.ds(0, WIDE)], s_a)

    @pl.when(group // 2 == core)
    def _():
        done(res.at[pl.ds(0, 3 * SLOTS * PART)], s_o)

    @pl.when(group // 2 != core)
    def _():
        done(res, s_o)

    done(att_out, a_sem)
    done(proj_out, o_sem)


def body(queries, keys, values, q_gain, k_gain, clip_frames, out_weight):
    anywhere = pl.BlockSpec(memory_space=pl.ANY)
    vmem = pl.BlockSpec(memory_space=pltpu.VMEM)
    bf16, f32 = jnp.bfloat16, jnp.float32
    dma = pltpu.SemaphoreType.DMA
    attended, projected = pl.pallas_call(
        kernel,
        out_shape=(pltpu.VMEM((1, ROWS, WIDE), bf16), pltpu.VMEM((1, ROWS, 2 * WIDE), bf16)),
        in_specs=[pl.BlockSpec(memory_space=pltpu.SMEM), anywhere, anywhere, anywhere, vmem, vmem, anywhere],
        out_specs=(vmem, vmem),
        scratch_shapes=[
            pltpu.VMEM((ROWS, WIDE), bf16),
            pltpu.VMEM((ROWS, WIDE), bf16),
            pltpu.VMEM((ROWS, WIDE), bf16),
            pltpu.VMEM((ROWS, WIDE), bf16),
            pltpu.VMEM((2, ROWS, 128), f32),
            pltpu.VMEM((CHUNKS, BLOCK, 256), bf16),
            pltpu.VMEM((TOKENS, 256), bf16),
            pltpu.VMEM((TOKENS, 256), bf16),
            pltpu.VMEM((CHUNKS, BLOCK, 128), bf16),
            pltpu.VMEM((SLOTS, 4 * PART, HD), bf16),
            pltpu.VMEM((HD, WIDE), bf16),
            pltpu.VMEM((SLOTS * 4 * PART, WIDE), bf16),
            dma((3,)), dma, dma, dma, dma, dma((CHUNKS,)), dma((SLOTS,)), dma((SLOTS,)), dma((SLOTS,)), dma((SLOTS,)), dma, dma,
            dma, dma, dma, dma, dma, dma, dma, dma, dma, dma,
        ],
        compiler_params=pltpu.CompilerParams(
            collective_id=0, has_side_effects=True, vmem_limit_bytes=56 << 20
        ),
        cost_estimate=pl.CostEstimate(flops=3 * 10**9, bytes_accessed=8 << 20, transcendentals=4 << 20),
    )(clip_frames, queries, keys, values, q_gain, k_gain, out_weight)
    return attended, projected


def solution(mesh):
    in_specs = (
        P("clip", "seq", "head"),
        P("clip", "seq", "head"),
        P("clip", "seq", "head"),
        P("head"),
        P("head"),
        P("clip", None),
        P("head", "clip"),
    )
    out_specs = (P("clip", "seq", "head"), P("clip", "seq", "head"))
    return jax.shard_map(body, mesh=mesh, in_specs=in_specs, out_specs=out_specs, check_vma=False)
```

```python
import jax
import jax.numpy as jnp
from jax import lax
from jax.experimental import pallas as pl
from jax.experimental.pallas import tpu as pltpu
from jax.sharding import PartitionSpec as P

HEADS = 20
HEAD_DIM = 128
HD = HEADS * HEAD_DIM
TOK_FRAME = 32
CLIPS = 8
SEQ = 16
ROWS = 128
WIDE = 1280
HERE = WIDE // HEAD_DIM
PART = 16
CHUNKS = ROWS // PART
SLOTS = CHUNKS // 2
BLOCK = SEQ * PART
KEYS = 512
TOKENS = SEQ * ROWS
QUART = 384
NARROW = 256
LAG_HOME, LAG_OUT = 3, 8
STEP_FAR = 5
MASKED = -1e30
MESH = pl.DeviceIdType.MESH


def lanes(start, size=HEAD_DIM):
    return pl.ds(pl.multiple_of(start, 128), size)


def rows(start, size):
    return pl.ds(pl.multiple_of(start, 16), size)


def owner_of(core, head):
    turn = head // 4
    z = head % 4 + 2 * core * (head // 8)
    y = (z + turn * (1 + 2 * core)) % 4
    return z * 4 + y


def owned_by(core, place):
    z, y = place // 4, place % 4
    off = (y - z + 4) % 4
    turn = jnp.where(off == 0, 0, jnp.where(off == 2, 2, jnp.where(off == 1 + 2 * core, 1, -1)))
    last = z - 2 * core
    head = jnp.where(turn == 2, 8 + last, turn * 4 + z)
    good = (turn >= 0) & ((turn < 2) | ((last >= 0) & (last < 2)))
    return jnp.where(good, head, -1)


def kernel(
    lens, q_in, k_in, v_in, q_gain, k_gain, w_in, att_out, proj_out,
    qf, kf, qn, kn, sums, qx, kx, vx, back, ag, w2, w4, res, res4,
    load_sem, sum_sem, w_sem, v_sem, k_sem, q_sem, r_sem, near_sem, row_sem, o_sem, a_sem, f_sem, g_sem,
    s_sum, s_w, s_v, s_k, s_q, s_r, s_x, s_y, s_o, s_p, s_a, s_f, s_g,
):
    place, core, group = lax.axis_index("seq"), lax.axis_index("head"), lax.axis_index("clip")
    other = 1 - core
    mine = owned_by(core, place)
    owner = mine >= 0
    z, y = place // 4, place % 4
    left, right, far = (group + 3) % 4, (group + 1) % 4, (group + 2) % 4
    part = (y + z) % 4

    def row_peer(step):
        along_y = z * 4 + (y + step) % 4
        along_z = (z + step) % 4 * 4 + y
        return jnp.where(core == 0, along_y, along_z)


    loads = [
        pltpu.make_async_copy(q_in.at[0], qf, load_sem.at[0]),
        pltpu.make_async_copy(k_in.at[0], kf, load_sem.at[1]),
        pltpu.make_async_copy(w_in, w2.at[rows(core * WIDE, WIDE)], load_sem.at[2]),
    ]
    for load in loads:
        load.start()

    barrier = pltpu.get_barrier_semaphore()

    def greet_plane(i, carry):
        to = (place + i) % SEQ
        pl.semaphore_signal(barrier, inc=1, device_id=(to, core, group), device_id_type=MESH)
        return carry

    lax.fori_loop(1, SEQ, greet_plane, 0)
    pl.semaphore_signal(barrier, inc=1, device_id=(place, other, group), device_id_type=MESH)

    for to in (left, right, far):
        pl.semaphore_signal(barrier, inc=1, device_id=(place, core, to), device_id_type=MESH)
    loads[0].wait()
    loads[1].wait()
    q_float = qf[...].astype(jnp.float32)
    k_float = kf[...].astype(jnp.float32)
    sum_q = jnp.sum(q_float * q_float, axis=1, keepdims=True)
    sum_k = jnp.sum(k_float * k_float, axis=1, keepdims=True)
    low = lax.broadcasted_iota(jnp.int32, (ROWS, 128), 1) < 64
    sums[0] = jnp.where(low, sum_q, sum_k)
    pl.semaphore_wait(barrier, SEQ - 1 + 1 + 3)

    def to_owners(copies):
        def one(i, carry):
            head = (i + place) % HERE
            to = owner_of(core, head)

            @pl.when(to == place)
            def _():
                for src, dst, send, recv in copies(head):
                    pltpu.make_async_copy(src, dst, recv).start()

            @pl.when(to != place)
            def _():
                for src, dst, send, recv in copies(head):
                    pltpu.make_async_remote_copy(
                        src, dst, send, recv, device_id=(to, core, group), device_id_type=MESH
                    ).start()

            return carry

        lax.fori_loop(0, HERE, one, 0)

    own_rows = rows(place * ROWS, ROWS)
    to_owners(lambda head: [(v_in.at[0, :, lanes(head * 128)], vx.at[own_rows, pl.ds(0, 128)], s_v, v_sem)])

    give_sums = pltpu.make_async_remote_copy(
        sums.at[0], sums.at[1], s_sum, sum_sem, device_id=(place, other, group), device_id_type=MESH
    )
    give_sums.start()
    give_w = pltpu.make_async_remote_copy(
        w_in, w2.at[rows(core * WIDE, WIDE)], s_w, w_sem,
        device_id=(place, other, group), device_id_type=MESH,
    )
    give_w.start()
    my_rows = w4.at[rows(core * WIDE, WIDE)]
    give_far = pltpu.make_async_remote_copy(
        w_in.at[:, lanes(jnp.minimum(part * QUART, WIDE - QUART), QUART)], my_rows, s_f, f_sem,
        device_id=(place, core, far), device_id_type=MESH,
    )
    give_far.start()
    pass_far = pltpu.make_async_remote_copy(
        my_rows, my_rows, s_g, g_sem, device_id=(place, other, group), device_id_type=MESH
    )
    give_sums.wait()
    both = sums[0] + sums[1]
    k_rate = lax.rsqrt(both[:, 64:65] / HD + 1e-06)
    kn[...] = (kf[...].astype(jnp.float32) * k_rate * k_gain[...].reshape(1, WIDE)).astype(jnp.bfloat16)
    to_owners(lambda head: [(kn.at[:, lanes(head * 128)], kx.at[own_rows, pl.ds(0, 128)], s_k, k_sem)])
    q_rate = lax.rsqrt(both[:, 0:1] / HD + 1e-06)
    qn[...] = (qf[...].astype(jnp.float32) * q_rate * q_gain[...].reshape(1, WIDE)).astype(jnp.bfloat16)

    def send_q(chunk, carry):
        to_owners(
            lambda head: [
                (
                    qn.at[rows(chunk * PART, PART), lanes(head * 128)],
                    qx.at[chunk, rows(place * PART, PART), pl.ds(0, 128)],
                    s_q,
                    q_sem.at[chunk],
                )
            ]
        )
        return carry

    lax.fori_loop(0, CHUNKS, send_q, 0)

    @pl.when(owner)
    def _():
        lane = lax.broadcasted_iota(jnp.int32, (1, 128), 1)
        first = jnp.zeros((1, 128), jnp.int32)
        last = jnp.zeros((1, 128), jnp.int32)
        end = jnp.int32(0)
        for clip in range(CLIPS):
            first = jnp.where(lane == clip, end, first)
            end = end + lens[0, clip]
            last = jnp.where(lane == clip, end, last)
        one = jnp.ones((), jnp.float32)
        zero = jnp.zeros((), jnp.float32)
        frame = lax.broadcasted_iota(jnp.int32, (TOKENS, 128), 0) // TOK_FRAME
        kx[:, 128:256] = jnp.where((frame >= first) & (frame < last), one, zero).astype(jnp.bfloat16)
        vx[:, 128:256] = jnp.ones((TOKENS, 128), jnp.bfloat16)
        for chunk in range(CHUNKS):
            frame = lax.broadcasted_iota(jnp.int32, (BLOCK, 128), 0) // PART * (ROWS // TOK_FRAME) + chunk * PART // TOK_FRAME
            off = jnp.logical_not((frame >= first) & (frame < last)) & (lane < CLIPS)
            qx[chunk, :, 128:256] = jnp.where(off, MASKED * one, zero).astype(jnp.bfloat16)
        pltpu.make_async_copy(vx.at[:, pl.ds(0, 128)], vx.at[:, pl.ds(0, 128)], v_sem).wait()
        pltpu.make_async_copy(kx.at[:, pl.ds(0, 128)], kx.at[:, pl.ds(0, 128)], k_sem).wait()

    loads[2].wait()
    give_w.wait()
    factor = HEAD_DIM ** (-0.5) * 1.4426950408889634

    def step(t, carry):
        @pl.when(owner & (t < CHUNKS))
        def _():
            chunk = t
            pltpu.make_async_copy(
                qx.at[chunk, :, pl.ds(0, 128)], qx.at[chunk, :, pl.ds(0, 128)], q_sem.at[chunk]
            ).wait()

            queries = qx[chunk]
            best, summed = None, None
            for first in range(0, TOKENS, KEYS):
                span = pl.ds(first, KEYS)
                score = lax.dot_general(
                    queries, kx[span, :], (((1,), (1,)), ((), ())), preferred_element_type=jnp.float32
                )
                top = jnp.max(score, axis=1, keepdims=True)
                if first:
                    top = jnp.maximum(best, top)
                weights = jnp.exp2((score - top) * factor).astype(jnp.bfloat16)
                added = jnp.dot(weights, vx[span, :], preferred_element_type=jnp.float32)
                summed = summed * jnp.exp2((best - top) * factor) + added if first else added
                best = top
            back[chunk] = (summed[:, :128] / summed[:, 128:]).astype(jnp.bfloat16)

            to_core = chunk % 2

            def give(i, carry):
                to = (place + i) % SEQ
                src = back.at[chunk, rows(to * PART, PART)]
                dst = ag.at[chunk // 2, pl.ds(2 * PART, PART), lanes((core * HERE + mine) * 128)]
                here = (i == 0) & (to_core == core)

                @pl.when(here)
                def _():
                    pltpu.make_async_copy(src, dst, r_sem.at[chunk // 2]).start()

                @pl.when(jnp.logical_not(here))
                def _():
                    pltpu.make_async_remote_copy(
                        src, dst, s_r, r_sem.at[chunk // 2], device_id=(to, to_core, group), device_id_type=MESH
                    ).start()

                return carry

            lax.fori_loop(0, SEQ, give, 0)

        def slot_of(lag):
            chunk = t - lag
            return chunk // 2, (chunk >= 0) & (chunk < CHUNKS) & (chunk % 2 == core)

        slot_home, now_home = slot_of(LAG_HOME)

        @pl.when(now_home)
        def _():
            block = ag.at[slot_home, pl.ds(2 * PART, PART)]
            pltpu.make_async_copy(block, block, r_sem.at[slot_home]).wait()
            for i, to in enumerate((right, left)):
                pltpu.make_async_remote_copy(
                    block, ag.at[slot_home, pl.ds(i * PART, PART)], s_x, near_sem.at[slot_home],
                    device_id=(place, core, to), device_id_type=MESH,
                ).start()
            for i in range(1, 4):
                pltpu.make_async_remote_copy(
                    block, ag.at[slot_home, pl.ds((2 + i) * PART, PART)], s_y, row_sem.at[slot_home],
                    device_id=(row_peer(i), core, group), device_id_type=MESH,
                ).start()
            rest = att_out.at[0, rows((2 * slot_home + core) * PART, PART)]
            pltpu.make_async_remote_copy(
                block.at[:, lanes(other * WIDE, WIDE)], rest, s_a, a_sem,
                device_id=(place, other, group), device_id_type=MESH,
            ).start()
            pltpu.make_async_copy(block.at[:, lanes(core * WIDE, WIDE)], rest, a_sem).start()

        @pl.when(t == STEP_FAR)
        def _():
            give_far.wait()
            pass_far.start()

        @pl.when(t == LAG_OUT)
        def _():
            pass_far.wait()

        slot_out, now_out = slot_of(LAG_OUT)

        @pl.when(now_out)
        def _():
            token_rows = rows((2 * slot_out + core) * PART, PART)

            two = ag.at[slot_out, pl.ds(0, 2 * PART)]
            pltpu.make_async_copy(two, two, near_sem.at[slot_out]).wait()
            total = jnp.dot(ag[slot_out, 0 : 3 * PART, :], w2[...], preferred_element_type=jnp.float32)
            res[slot_out] = total.astype(jnp.bfloat16)
            to_core = group // 2
            dst = proj_out.at[0, token_rows, lanes((group % 2) * WIDE, WIDE)]
            for i, to in enumerate((left, right)):
                pltpu.make_async_remote_copy(
                    res.at[slot_out, pl.ds(i * PART, PART)], dst, s_o, o_sem,
                    device_id=(place, to_core, to), device_id_type=MESH,
                ).start()
            src = res.at[slot_out, pl.ds(2 * PART, PART)]

            @pl.when(to_core == core)
            def _():
                pltpu.make_async_copy(src, dst, o_sem).start()

            @pl.when(to_core != core)
            def _():
                pltpu.make_async_remote_copy(
                    src, dst, s_o, o_sem, device_id=(place, to_core, group), device_id_type=MESH
                ).start()

            three = ag.at[slot_out, pl.ds(3 * PART, 3 * PART)]
            pltpu.make_async_copy(three, three, row_sem.at[slot_out]).wait()
            total = jnp.dot(ag[slot_out, 2 * PART :, :], w4[...], preferred_element_type=jnp.float32)
            res4[slot_out] = total.astype(jnp.bfloat16)
            far_core = far // 2

            def give_part(width, first, column):
                far_dst = proj_out.at[0, token_rows, lanes((far % 2) * WIDE + column, width)]
                for i in range(1, 4):
                    pltpu.make_async_remote_copy(
                        res4.at[slot_out, pl.ds(i * PART, PART), lanes(first, width)], far_dst, s_p, o_sem,
                        device_id=(row_peer(4 - i), far_core, group), device_id_type=MESH,
                    ).start()
                far_src = res4.at[slot_out, pl.ds(0, PART), lanes(first, width)]

                @pl.when(far_core == core)
                def _():
                    pltpu.make_async_copy(far_src, far_dst, o_sem).start()

                @pl.when(far_core != core)
                def _():
                    pltpu.make_async_remote_copy(
                        far_src, far_dst, s_p, o_sem, device_id=(place, far_core, group), device_id_type=MESH
                    ).start()

            @pl.when(part < 2)
            def _():
                give_part(QUART, 0, part * QUART)

            @pl.when(part >= 2)
            def _():
                give_part(NARROW, (part - 2) * 128, 2 * QUART + (part - 2) * NARROW)

        return carry

    lax.fori_loop(0, CHUNKS + LAG_OUT, step, 0)

    def done(ref, sem):
        pltpu.make_async_copy(ref, ref, sem).wait()

    @pl.when(owner)
    def _():
        for sem in (s_v, s_k, s_q):
            done(kn.at[:, pl.ds(0, 9 * 128)], sem)
        done(kx.at[pl.ds(0, TOKENS - ROWS // 2), pl.ds(0, 128)], s_r)

    @pl.when(jnp.logical_not(owner))
    def _():
        for sem in (s_v, s_k, s_q):
            done(kn, sem)

    done(ag.at[:, pl.ds(0, 2 * PART)], s_x)
    done(ag.at[:, pl.ds(0, 3 * PART)], s_y)
    done(ag.at[:, pl.ds(0, PART), pl.ds(0, WIDE)], s_a)

    for is_here, near_rows, far_rows in ((True, 2 * PART, 4 * PART), (False, 3 * PART, 3 * PART)):

        @pl.when((group // 2 == core) == is_here)
        def _(near_rows=near_rows, far_rows=far_rows):
            done(res.at[:, pl.ds(0, near_rows)], s_o)

            @pl.when(part < 2)
            def _():
                done(res4.at[:, pl.ds(0, far_rows)], s_p)

            @pl.when(part >= 2)
            def _():
                done(res4.at[:, pl.ds(0, far_rows), pl.ds(0, NARROW)], s_p)

    done(att_out, a_sem)
    done(proj_out, o_sem)


def body(queries, keys, values, q_gain, k_gain, clip_frames, out_weight):
    anywhere = pl.BlockSpec(memory_space=pl.ANY)
    vmem = pl.BlockSpec(memory_space=pltpu.VMEM)
    bf16, f32 = jnp.bfloat16, jnp.float32
    dma = pltpu.SemaphoreType.DMA
    attended, projected = pl.pallas_call(
        kernel,
        out_shape=(pltpu.VMEM((1, ROWS, WIDE), bf16), pltpu.VMEM((1, ROWS, 2 * WIDE), bf16)),
        in_specs=[pl.BlockSpec(memory_space=pltpu.SMEM), anywhere, anywhere, anywhere, vmem, vmem, anywhere],
        out_specs=(vmem, vmem),
        scratch_shapes=[
            pltpu.VMEM((ROWS, WIDE), bf16),
            pltpu.VMEM((ROWS, WIDE), bf16),
            pltpu.VMEM((ROWS, WIDE), bf16),
            pltpu.VMEM((ROWS, WIDE), bf16),
            pltpu.VMEM((2, ROWS, 128), f32),
            pltpu.VMEM((CHUNKS, BLOCK, 256), bf16),
            pltpu.VMEM((TOKENS, 256), bf16),
            pltpu.VMEM((TOKENS, 256), bf16),
            pltpu.VMEM((CHUNKS, BLOCK, 128), bf16),
            pltpu.VMEM((SLOTS, 6 * PART, HD), bf16),
            pltpu.VMEM((HD, WIDE), bf16),
            pltpu.VMEM((HD, QUART), bf16),
            pltpu.VMEM((SLOTS, 3 * PART, WIDE), bf16),
            pltpu.VMEM((SLOTS, 4 * PART, QUART), bf16),
            dma((3,)), dma, dma, dma, dma, dma((CHUNKS,)), dma((SLOTS,)), dma((SLOTS,)), dma((SLOTS,)), dma, dma, dma, dma,
            dma, dma, dma, dma, dma, dma, dma, dma, dma, dma, dma, dma, dma,
        ],
        compiler_params=pltpu.CompilerParams(
            collective_id=0, has_side_effects=True, vmem_limit_bytes=56 << 20
        ),
        cost_estimate=pl.CostEstimate(flops=3 * 10**9, bytes_accessed=8 << 20, transcendentals=4 << 20),
    )(clip_frames, queries, keys, values, q_gain, k_gain, out_weight)
    return attended, projected


def solution(mesh):
    in_specs = (
        P("clip", "seq", "head"),
        P("clip", "seq", "head"),
        P("clip", "seq", "head"),
        P("head"),
        P("head"),
        P("clip", None),
        P("head", "clip"),
    )
    out_specs = (P("clip", "seq", "head"), P("clip", "seq", "head"))
    return jax.shard_map(body, mesh=mesh, in_specs=in_specs, out_specs=out_specs, check_vma=False)
```

```python
import jax
import jax.numpy as jnp
from jax import lax
from jax.experimental import pallas as pl
from jax.experimental.pallas import tpu as pltpu
from jax.sharding import PartitionSpec as P

HEADS = 20
HEAD_DIM = 128
HD = HEADS * HEAD_DIM
TOK_FRAME = 32
CLIPS = 8
SEQ = 16
ROWS = 128
WIDE = 1280
HERE = WIDE // HEAD_DIM
PART = 16
CHUNKS = ROWS // PART
SLOTS = CHUNKS // 2
BLOCK = SEQ * PART
KEYS = 512
TOKENS = SEQ * ROWS
QUART = 384
NARROW = 256
LAG_HOME, LAG_OUT = 3, 7
STEP_FAR = 4
MASKED = -1e30
MESH = pl.DeviceIdType.MESH


def lanes(start, size=HEAD_DIM):
    return pl.ds(pl.multiple_of(start, 128), size)


def rows(start, size):
    return pl.ds(pl.multiple_of(start, 16), size)


def owner_of(core, head):
    turn = head // 4
    z = head % 4 + 2 * core * (head // 8)
    y = (z + turn * (1 + 2 * core)) % 4
    return z * 4 + y


def owned_by(core, place):
    z, y = place // 4, place % 4
    off = (y - z + 4) % 4
    turn = jnp.where(off == 0, 0, jnp.where(off == 2, 2, jnp.where(off == 1 + 2 * core, 1, -1)))
    last = z - 2 * core
    head = jnp.where(turn == 2, 8 + last, turn * 4 + z)
    good = (turn >= 0) & ((turn < 2) | ((last >= 0) & (last < 2)))
    return jnp.where(good, head, -1)


def kernel(
    lens, q_in, k_in, v_in, q_gain, k_gain, w_in, att_out, proj_out,
    qf, kf, qn, kn, sums, qx, kx, vx, back, ag, w2, w4, res, res4,
    load_sem, sum_sem, w_sem, v_sem, k_sem, q_sem, r_sem, near_sem, row_sem, o_sem, a_sem, f_sem, g_sem,
    s_sum, s_w, s_v, s_k, s_q, s_r, s_x, s_y, s_o, s_p, s_a, s_f, s_g,
):
    place, core, group = lax.axis_index("seq"), lax.axis_index("head"), lax.axis_index("clip")
    other = 1 - core
    mine = owned_by(core, place)
    owner = mine >= 0
    z, y = place // 4, place % 4
    left, right, far = (group + 3) % 4, (group + 1) % 4, (group + 2) % 4
    part = (y + z) % 4

    def row_peer(step):
        along_y = z * 4 + (y + step) % 4
        along_z = (z + step) % 4 * 4 + y
        return jnp.where(core == 0, along_y, along_z)


    loads = [
        pltpu.make_async_copy(q_in.at[0], qf, load_sem.at[0]),
        pltpu.make_async_copy(k_in.at[0], kf, load_sem.at[1]),
        pltpu.make_async_copy(w_in, w2.at[rows(core * WIDE, WIDE)], load_sem.at[2]),
    ]
    for load in loads:
        load.start()

    barrier = pltpu.get_barrier_semaphore()

    def greet_plane(i, carry):
        to = (place + i) % SEQ
        pl.semaphore_signal(barrier, inc=1, device_id=(to, core, group), device_id_type=MESH)
        return carry

    lax.fori_loop(1, SEQ, greet_plane, 0)
    pl.semaphore_signal(barrier, inc=1, device_id=(place, other, group), device_id_type=MESH)

    for to in (left, right, far):
        pl.semaphore_signal(barrier, inc=1, device_id=(place, core, to), device_id_type=MESH)
    loads[0].wait()
    loads[1].wait()
    q_float = qf[...].astype(jnp.float32)
    k_float = kf[...].astype(jnp.float32)
    sum_q = jnp.sum(q_float * q_float, axis=1, keepdims=True)
    sum_k = jnp.sum(k_float * k_float, axis=1, keepdims=True)
    low = lax.broadcasted_iota(jnp.int32, (ROWS, 128), 1) < 64
    sums[0] = jnp.where(low, sum_q, sum_k)
    pl.semaphore_wait(barrier, SEQ - 1 + 1 + 3)

    def to_owners(copies):
        def one(i, carry):
            head = (3 * i + place) % HERE
            to = owner_of(core, head)

            @pl.when(to == place)
            def _():
                for src, dst, send, recv in copies(head):
                    pltpu.make_async_copy(src, dst, recv).start()

            @pl.when(to != place)
            def _():
                for src, dst, send, recv in copies(head):
                    pltpu.make_async_remote_copy(
                        src, dst, send, recv, device_id=(to, core, group), device_id_type=MESH
                    ).start()

            return carry

        lax.fori_loop(0, HERE, one, 0)

    own_rows = rows(place * ROWS, ROWS)
    to_owners(lambda head: [(v_in.at[0, :, lanes(head * 128)], vx.at[own_rows, pl.ds(0, 128)], s_v, v_sem)])

    give_sums = pltpu.make_async_remote_copy(
        sums.at[0], sums.at[1], s_sum, sum_sem, device_id=(place, other, group), device_id_type=MESH
    )
    give_sums.start()
    give_w = pltpu.make_async_remote_copy(
        w_in, w2.at[rows(core * WIDE, WIDE)], s_w, w_sem,
        device_id=(place, other, group), device_id_type=MESH,
    )
    give_w.start()
    my_rows = w4.at[rows(core * WIDE, WIDE)]
    give_far = pltpu.make_async_remote_copy(
        w_in.at[:, lanes(jnp.minimum(part * QUART, WIDE - QUART), QUART)], my_rows, s_f, f_sem,
        device_id=(place, core, far), device_id_type=MESH,
    )
    give_far.start()
    pass_far = pltpu.make_async_remote_copy(
        my_rows, my_rows, s_g, g_sem, device_id=(place, other, group), device_id_type=MESH
    )
    give_sums.wait()
    both = sums[0] + sums[1]
    k_rate = lax.rsqrt(both[:, 64:65] / HD + 1e-06)
    kn[...] = (kf[...].astype(jnp.float32) * k_rate * k_gain[...].reshape(1, WIDE)).astype(jnp.bfloat16)
    to_owners(lambda head: [(kn.at[:, lanes(head * 128)], kx.at[own_rows, pl.ds(0, 128)], s_k, k_sem)])
    q_rate = lax.rsqrt(both[:, 0:1] / HD + 1e-06)
    qn[...] = (qf[...].astype(jnp.float32) * q_rate * q_gain[...].reshape(1, WIDE)).astype(jnp.bfloat16)

    def send_q(chunk, carry):
        to_owners(
            lambda head: [
                (
                    qn.at[rows(chunk * PART, PART), lanes(head * 128)],
                    qx.at[chunk, rows(place * PART, PART), pl.ds(0, 128)],
                    s_q,
                    q_sem.at[chunk],
                )
            ]
        )
        return carry

    lax.fori_loop(0, CHUNKS, send_q, 0)

    @pl.when(owner)
    def _():
        lane = lax.broadcasted_iota(jnp.int32, (1, 128), 1)
        first = jnp.zeros((1, 128), jnp.int32)
        last = jnp.zeros((1, 128), jnp.int32)
        end = jnp.int32(0)
        for clip in range(CLIPS):
            first = jnp.where(lane == clip, end, first)
            end = end + lens[0, clip]
            last = jnp.where(lane == clip, end, last)
        one = jnp.ones((), jnp.float32)
        zero = jnp.zeros((), jnp.float32)
        frame = lax.broadcasted_iota(jnp.int32, (TOKENS, 128), 0) // TOK_FRAME
        kx[:, 128:256] = jnp.where((frame >= first) & (frame < last), one, zero).astype(jnp.bfloat16)
        vx[:, 128:256] = jnp.ones((TOKENS, 128), jnp.bfloat16)
        for chunk in range(CHUNKS):
            frame = lax.broadcasted_iota(jnp.int32, (BLOCK, 128), 0) // PART * (ROWS // TOK_FRAME) + chunk * PART // TOK_FRAME
            off = jnp.logical_not((frame >= first) & (frame < last)) & (lane < CLIPS)
            qx[chunk, :, 128:256] = jnp.where(off, MASKED * one, zero).astype(jnp.bfloat16)
        pltpu.make_async_copy(vx.at[:, pl.ds(0, 128)], vx.at[:, pl.ds(0, 128)], v_sem).wait()
        pltpu.make_async_copy(kx.at[:, pl.ds(0, 128)], kx.at[:, pl.ds(0, 128)], k_sem).wait()

    factor = HEAD_DIM ** (-0.5) * 1.4426950408889634

    def step(t, carry):
        @pl.when(owner & (t < CHUNKS))
        def _():
            chunk = t
            pltpu.make_async_copy(
                qx.at[chunk, :, pl.ds(0, 128)], qx.at[chunk, :, pl.ds(0, 128)], q_sem.at[chunk]
            ).wait()

            queries = qx[chunk]
            best, summed = None, None
            for first in range(0, TOKENS, KEYS):
                span = pl.ds(first, KEYS)
                score = lax.dot_general(
                    queries, kx[span, :], (((1,), (1,)), ((), ())), preferred_element_type=jnp.float32
                )
                top = jnp.max(score, axis=1, keepdims=True)
                if first:
                    top = jnp.maximum(best, top)
                weights = jnp.exp2((score - top) * factor).astype(jnp.bfloat16)
                added = jnp.dot(weights, vx[span, :], preferred_element_type=jnp.float32)
                summed = summed * jnp.exp2((best - top) * factor) + added if first else added
                best = top
            back[chunk] = (summed[:, :128] / summed[:, 128:]).astype(jnp.bfloat16)

            to_core = chunk % 2

            def give(i, carry):
                to = (place + i) % SEQ
                src = back.at[chunk, rows(to * PART, PART)]
                dst = ag.at[chunk // 2, pl.ds(2 * PART, PART), lanes((core * HERE + mine) * 128)]
                here = (i == 0) & (to_core == core)

                @pl.when(here)
                def _():
                    pltpu.make_async_copy(src, dst, r_sem.at[chunk // 2]).start()

                @pl.when(jnp.logical_not(here))
                def _():
                    pltpu.make_async_remote_copy(
                        src, dst, s_r, r_sem.at[chunk // 2], device_id=(to, to_core, group), device_id_type=MESH
                    ).start()

                return carry

            lax.fori_loop(0, SEQ, give, 0)

        def slot_of(lag):
            chunk = t - lag
            return chunk // 2, (chunk >= 0) & (chunk < CHUNKS) & (chunk % 2 == core)

        slot_home, now_home = slot_of(LAG_HOME)

        @pl.when(now_home)
        def _():
            block = ag.at[slot_home, pl.ds(2 * PART, PART)]
            pltpu.make_async_copy(block, block, r_sem.at[slot_home]).wait()
            for i, to in enumerate((right, left)):
                pltpu.make_async_remote_copy(
                    block, ag.at[slot_home, pl.ds(i * PART, PART)], s_x, near_sem.at[slot_home],
                    device_id=(place, core, to), device_id_type=MESH,
                ).start()
            for i in range(1, 4):
                pltpu.make_async_remote_copy(
                    block, ag.at[slot_home, pl.ds((2 + i) * PART, PART)], s_y, row_sem.at[slot_home],
                    device_id=(row_peer(i), core, group), device_id_type=MESH,
                ).start()
            rest = att_out.at[0, rows((2 * slot_home + core) * PART, PART)]
            pltpu.make_async_remote_copy(
                block.at[:, lanes(other * WIDE, WIDE)], rest, s_a, a_sem,
                device_id=(place, other, group), device_id_type=MESH,
            ).start()
            pltpu.make_async_copy(block.at[:, lanes(core * WIDE, WIDE)], rest, a_sem).start()

        @pl.when(t == STEP_FAR)
        def _():
            give_far.wait()
            pass_far.start()

        @pl.when(t == LAG_OUT)
        def _():
            loads[2].wait()
            give_w.wait()
            pass_far.wait()

        slot_out, now_out = slot_of(LAG_OUT)

        @pl.when(now_out)
        def _():
            token_rows = rows((2 * slot_out + core) * PART, PART)

            two = ag.at[slot_out, pl.ds(0, 2 * PART)]
            pltpu.make_async_copy(two, two, near_sem.at[slot_out]).wait()
            total = jnp.dot(ag[slot_out, 0 : 3 * PART, :], w2[...], preferred_element_type=jnp.float32)
            res[slot_out] = total.astype(jnp.bfloat16)
            to_core = group // 2
            dst = proj_out.at[0, token_rows, lanes((group % 2) * WIDE, WIDE)]
            for i, to in enumerate((left, right)):
                pltpu.make_async_remote_copy(
                    res.at[slot_out, pl.ds(i * PART, PART)], dst, s_o, o_sem,
                    device_id=(place, to_core, to), device_id_type=MESH,
                ).start()
            src = res.at[slot_out, pl.ds(2 * PART, PART)]

            @pl.when(to_core == core)
            def _():
                pltpu.make_async_copy(src, dst, o_sem).start()

            @pl.when(to_core != core)
            def _():
                pltpu.make_async_remote_copy(
                    src, dst, s_o, o_sem, device_id=(place, to_core, group), device_id_type=MESH
                ).start()

            three = ag.at[slot_out, pl.ds(3 * PART, 3 * PART)]
            pltpu.make_async_copy(three, three, row_sem.at[slot_out]).wait()
            total = jnp.dot(ag[slot_out, 2 * PART :, :], w4[...], preferred_element_type=jnp.float32)
            res4[slot_out] = total.astype(jnp.bfloat16)
            far_core = far // 2

            def give_part(width, first, column):
                far_dst = proj_out.at[0, token_rows, lanes((far % 2) * WIDE + column, width)]
                for i in range(1, 4):
                    pltpu.make_async_remote_copy(
                        res4.at[slot_out, pl.ds(i * PART, PART), lanes(first, width)], far_dst, s_p, o_sem,
                        device_id=(row_peer(4 - i), far_core, group), device_id_type=MESH,
                    ).start()
                far_src = res4.at[slot_out, pl.ds(0, PART), lanes(first, width)]

                @pl.when(far_core == core)
                def _():
                    pltpu.make_async_copy(far_src, far_dst, o_sem).start()

                @pl.when(far_core != core)
                def _():
                    pltpu.make_async_remote_copy(
                        far_src, far_dst, s_p, o_sem, device_id=(place, far_core, group), device_id_type=MESH
                    ).start()

            @pl.when(part < 2)
            def _():
                give_part(QUART, 0, part * QUART)

            @pl.when(part >= 2)
            def _():
                give_part(NARROW, (part - 2) * 128, 2 * QUART + (part - 2) * NARROW)

        return carry

    lax.fori_loop(0, CHUNKS + LAG_OUT, step, 0)

    def done(ref, sem):
        pltpu.make_async_copy(ref, ref, sem).wait()

    @pl.when(owner)
    def _():
        for sem in (s_v, s_k, s_q):
            done(kn.at[:, pl.ds(0, 9 * 128)], sem)
        done(kx.at[pl.ds(0, TOKENS - ROWS // 2), pl.ds(0, 128)], s_r)

    @pl.when(jnp.logical_not(owner))
    def _():
        for sem in (s_v, s_k, s_q):
            done(kn, sem)

    done(ag.at[:, pl.ds(0, 2 * PART)], s_x)
    done(ag.at[:, pl.ds(0, 3 * PART)], s_y)
    done(ag.at[:, pl.ds(0, PART), pl.ds(0, WIDE)], s_a)

    for is_here, near_rows, far_rows in ((True, 2 * PART, 4 * PART), (False, 3 * PART, 3 * PART)):

        @pl.when((group // 2 == core) == is_here)
        def _(near_rows=near_rows, far_rows=far_rows):
            done(res.at[:, pl.ds(0, near_rows)], s_o)

            @pl.when(part < 2)
            def _():
                done(res4.at[:, pl.ds(0, far_rows)], s_p)

            @pl.when(part >= 2)
            def _():
                done(res4.at[:, pl.ds(0, far_rows), pl.ds(0, NARROW)], s_p)

    done(att_out, a_sem)
    done(proj_out, o_sem)


def body(queries, keys, values, q_gain, k_gain, clip_frames, out_weight):
    anywhere = pl.BlockSpec(memory_space=pl.ANY)
    vmem = pl.BlockSpec(memory_space=pltpu.VMEM)
    bf16, f32 = jnp.bfloat16, jnp.float32
    dma = pltpu.SemaphoreType.DMA
    attended, projected = pl.pallas_call(
        kernel,
        out_shape=(pltpu.VMEM((1, ROWS, WIDE), bf16), pltpu.VMEM((1, ROWS, 2 * WIDE), bf16)),
        in_specs=[pl.BlockSpec(memory_space=pltpu.SMEM), anywhere, anywhere, anywhere, vmem, vmem, anywhere],
        out_specs=(vmem, vmem),
        scratch_shapes=[
            pltpu.VMEM((ROWS, WIDE), bf16),
            pltpu.VMEM((ROWS, WIDE), bf16),
            pltpu.VMEM((ROWS, WIDE), bf16),
            pltpu.VMEM((ROWS, WIDE), bf16),
            pltpu.VMEM((2, ROWS, 128), f32),
            pltpu.VMEM((CHUNKS, BLOCK, 256), bf16),
            pltpu.VMEM((TOKENS, 256), bf16),
            pltpu.VMEM((TOKENS, 256), bf16),
            pltpu.VMEM((CHUNKS, BLOCK, 128), bf16),
            pltpu.VMEM((SLOTS, 6 * PART, HD), bf16),
            pltpu.VMEM((HD, WIDE), bf16),
            pltpu.VMEM((HD, QUART), bf16),
            pltpu.VMEM((SLOTS, 3 * PART, WIDE), bf16),
            pltpu.VMEM((SLOTS, 4 * PART, QUART), bf16),
            dma((3,)), dma, dma, dma, dma, dma((CHUNKS,)), dma((SLOTS,)), dma((SLOTS,)), dma((SLOTS,)), dma, dma, dma, dma,
            dma, dma, dma, dma, dma, dma, dma, dma, dma, dma, dma, dma, dma,
        ],
        compiler_params=pltpu.CompilerParams(
            collective_id=0, has_side_effects=True, vmem_limit_bytes=56 << 20
        ),
        cost_estimate=pl.CostEstimate(flops=3 * 10**9, bytes_accessed=8 << 20, transcendentals=4 << 20),
    )(clip_frames, queries, keys, values, q_gain, k_gain, out_weight)
    return attended, projected


def solution(mesh):
    in_specs = (
        P("clip", "seq", "head"),
        P("clip", "seq", "head"),
        P("clip", "seq", "head"),
        P("head"),
        P("head"),
        P("clip", None),
        P("head", "clip"),
    )
    out_specs = (P("clip", "seq", "head"), P("clip", "seq", "head"))
    return jax.shard_map(body, mesh=mesh, in_specs=in_specs, out_specs=out_specs, check_vma=False)
```
